32 devices in a mesh: groups: 2 (over y), query: 4 (over z), dim: 4 (over x, core).
Axes of the slice: x: 2, y: 2, z: 4, core: 2. Of those that a mesh axis runs over, the one named last changes fastest.
Arguments:
- query_grads: float32 [64, 262144], P('query', 'dim'), may hold values from -6 to 6
- train_grads: bfloat16 [128, 262144], P(('groups', 'query'), 'dim'), parts along dimension 0, may hold values from -0.01171875 to 0.01171875
- example_ids: int32 [128], P(('groups', 'query')), parts along dimension 0, may hold values from 0 to 4095
- query_ids: int32 [64], P(('query', 'dim')), may hold values from 0 to 4095
- query_norms: float32 [4096], replicated, may hold values from 0.3 to 3
- train_norms: float32 [8192], P('groups'), parts along dimension 0, may hold values from 0.3 to 3
Outputs:
- scores: float32 [128, 64], P(('groups', 'query', 'dim')), parts along dimension 0
The draws below stay inside these ranges and needn't reach their ends.
There are 2 independent parts, one for each index of `groups`. The reference program is written for one: setup_inputs(seed, part) draws one part's arguments, and reference() takes and returns one part's arrays. A program takes and returns all parts, laid end to end along the dimension named above; an argument that names none is the same for every part. Nothing has to cross between parts.
All inputs are finite; a program needn't handle non-finite values.
Results may differ from the reference program's by a relative error of at most 0.0003.
Values may be sent and summed in bfloat16 or wider, within the bound.
A program may use at most 64 MiB of HBM per device.

```python
import math
import jax
import jax.numpy as jnp
from jax import lax

G = 262144
QD = 16
CH = 16
STEPS = 4
EX = 4096
NQT = 4096
NQ = 64
TRAIN_ROWS = 64
N_QUERY = 4


def touch_ends(result, rng, low, top_value):
    shape = result.shape
    index_at = [jax.random.randint(jax.random.fold_in(rng, axis), (), 0, shape[axis]) for axis in range(len(shape))]
    result = result.at[tuple(index_at)].set(low)
    longest = shape.index(max(shape))
    index_at[longest] = (index_at[longest] + 1) % shape[longest]
    return result.at[tuple(index_at)].set(top_value)


def steps_of(rng, shape, split, smallest, largest):
    factor_of = 1.0
    for axis_at, shards_of in split:
        steps = jax.random.uniform(jax.random.fold_in(jax.random.fold_in(rng, 6), axis_at), (shards_of,), jnp.float32, smallest / len(split), largest / len(split))
        factor_of = factor_of * jnp.repeat(jnp.exp(steps), shape[axis_at] // shards_of).reshape((-1,) + (1,) * (len(shape) - 1 - axis_at))
    return factor_of


def centred(own_key, dims, scale, most, cuts=(), held_as=jnp.bfloat16):
    factor_of = steps_of(own_key, dims, cuts, -0.22, 0.18) if cuts else 1.0
    values = jax.random.normal(own_key, dims, jnp.float32) * scale * factor_of
    return jnp.minimum(jnp.maximum(values, -most), most).astype(held_as)


def setup_inputs(seed: int = 0, part: int = 0) -> dict:
    key_list = jax.random.split(jax.random.key(seed), 7)
    part_keys = jax.random.split(jax.random.fold_in(key_list[6], part), 7)
    return {
        "query_grads": centred(key_list[0], (NQ, G), 1.0, 6.0, ((0, 4), (1, 4)), jnp.float32),
        "train_grads": centred(part_keys[1], (TRAIN_ROWS, G), G ** -0.5, 0.01171875, ((0, 4), (1, 4))),
        "example_ids": touch_ends(jax.random.randint(part_keys[2], (TRAIN_ROWS,), 0, EX), jax.random.fold_in(part_keys[2], 1), 0, EX - 1).astype(jnp.int32),
        "query_ids": touch_ends(jax.random.randint(key_list[3], (NQ,), 0, NQT), jax.random.fold_in(key_list[3], 1), 0, NQT - 1).astype(jnp.int32),
        "query_norms": jnp.clip(jnp.exp(jax.random.uniform(key_list[4], (NQT,), jnp.float32, math.log(0.3), math.log(3.0))), 0.3, 3.0),
        "train_norms": jnp.clip(jnp.exp(jax.random.uniform(part_keys[5], (EX,), jnp.float32, math.log(0.3), math.log(3.0))), 0.3, 3.0),
    }


def reference(query_grads, train_grads, example_ids, query_ids, query_norms, train_norms):
    queries = query_grads.reshape(N_QUERY, QD, G)
    blocks = train_grads.reshape(N_QUERY, CH, G)
    block_ids = example_ids.reshape(N_QUERY, CH)

    def one_block(index):
        rows = lax.dynamic_index_in_dim(queries, index, 0, keepdims=False)
        pieces = []
        id_pieces = []
        for offset in range(STEPS):
            source = ((index - offset) % N_QUERY).astype(jnp.int32)
            span = lax.dynamic_index_in_dim(blocks, source, 0, keepdims=False).astype(jnp.float32)
            pieces.append(lax.dot_general(rows, span, (((1,), (1,)), ((), ())), precision=lax.Precision.HIGHEST, preferred_element_type=jnp.float32))
            id_pieces.append(lax.dynamic_index_in_dim(block_ids, source, 0, keepdims=False))
        return jnp.concatenate(pieces, axis=1), jnp.concatenate(id_pieces, axis=0)

    raw, seen_ids = lax.map(one_block, jnp.arange(N_QUERY, dtype=jnp.int32))
    train_scale = train_norms[seen_ids]
    query_scale = query_norms[query_ids].reshape(N_QUERY, QD, 1)
    scores = raw / (query_scale * train_scale[:, None, :])
    return scores.reshape(NQ, STEPS * CH)
```

```python
import functools

import jax
import jax.numpy as jnp
from jax import lax
from jax.experimental import pallas as pl
from jax.experimental.pallas import tpu as pltpu
from jax.sharding import PartitionSpec as P

STEPS = 4
WIDTH = 2048
FULL = 32767.0
MESH = pl.DeviceIdType.MESH


def passed_along(value, axis, by):
    size = lax.axis_size(axis)
    return lax.ppermute(value, axis, [(i, (i + by) % size) for i in range(size)])


def partial_scores(queries, span):
    return lax.dot_general(
        queries,
        span.astype(jnp.float32),
        (((1,), (1,)), ((), ())),
        precision=lax.Precision.HIGHEST,
        preferred_element_type=jnp.float32,
    )


def lookup(table, indices):
    matches = indices[:, None] == lax.iota(jnp.int32, table.shape[0])[None, :]
    return jnp.sum(jnp.where(matches, table[None, :], 0.0), axis=1)


def on_device(query_grads, train_grads, example_ids, query_ids, query_norms, train_norms):
    visited = [(train_grads, example_ids)]
    current = train_grads
    current_ids = example_ids
    for offset in range(1, STEPS):
        current, current_ids = passed_along((current, current_ids), "query", 1)
        visited.append((current, current_ids))
    partials = [partial_scores(query_grads, span) for span, span_ids in visited]
    summed = jnp.concatenate(
        [lax.psum_scatter(piece, "dim", scatter_dimension=0, tiled=True) for piece in partials],
        axis=1,
    )
    seen_ids = jnp.concatenate([span_ids for span, span_ids in visited], axis=0)
    train_scale = lookup(train_norms, seen_ids)
    query_scale = lookup(query_norms, query_ids)
    return summed / (query_scale[:, None] * train_scale[None, :])


def kernel(
    sizes, width, wide,
    q_ref, t_ref, eid_ref, qid_ref, qn_ref, tn_ref, out_ref,
    qf, code, tb, acc, scales, part, part_in, final, final_in,
    local_sem, own_send, fwd_send, q_recv, t_send, t_recv,
    scale_send, scale_recv, part_send, part_recv, final_send, final_recv,
):
    groups, steps, dims = sizes
    rows = q_ref.shape[0]
    mine = rows // dims
    half = qf.shape[1]
    chunks = half // width
    y, z, d = lax.axis_index("groups"), lax.axis_index("query"), lax.axis_index("dim")
    other_y = 1 - y
    high = z // 2
    is_inner = jnp.logical_or(z == 1, z == 2)
    partner = jnp.where(high == 0, 1 - z, 5 - z)
    end = jnp.where(high == 0, 0, 3)
    far_inner = jnp.where(high == 0, 2, 1)
    far_end = jnp.where(high == 0, 3, 0)
    plane = groups * dims
    place = y * dims + d

    def cols(c, base=0):
        return pl.ds(pl.multiple_of(base + c * width, width), width)

    def remote(src, dst, send, recv, to):
        return pltpu.make_async_remote_copy(
            src_ref=src, dst_ref=dst, send_sem=send, recv_sem=recv,
            device_id=to, device_id_type=MESH,
        )

    def send_code(block, c, to_z, send):
        view = code.at[block, :, cols(c)]
        return remote(view, view, send, q_recv.at[block, c], (y, to_z, d))

    def got_code(block, c):
        send_code(block, c, partner, own_send.at[0, c]).wait_recv()

    def send_train(c, half_of, slot, send, to):
        return remote(
            t_ref.at[:, cols(c, half_of * half)],
            tb.at[pl.ds(pl.multiple_of(slot * rows, rows), rows), cols(c)],
            send, t_recv.at[slot, c], to,
        )

    def got_train(slot, c):
        send_train(c, y, slot, t_send.at[0, c], (y, partner, d)).wait_recv()

    across = [(c, other_y, y, t_send.at[0, c], (other_y, z, d)) for c in range(chunks)]
    diagonal = [(c, other_y, 2 + y, t_send.at[0, c], (other_y, partner, d)) for c in range(chunks)]
    straight = [(c, y, 2 + y, t_send.at[1, c], (y, partner, d)) for c in range(chunks)]

    load_q = pltpu.make_async_copy(
        q_ref.at[:, pl.ds(pl.multiple_of(y * half, half), half)], qf, local_sem.at[0])
    load_t = pltpu.make_async_copy(
        t_ref.at[:, pl.ds(pl.multiple_of(y * half, half), half)],
        tb.at[pl.ds(pl.multiple_of(y * rows, rows), rows), :], local_sem.at[1])
    load_q.start()
    load_t.start()

    barrier = pltpu.get_barrier_semaphore()
    peers = []
    for step in range(1, plane):
        at = lax.rem(place + step, plane)
        peers.append((at // dims, z, lax.rem(at, dims)))
    for step in range(1, steps):
        peers.append((y, lax.rem(z + step, steps), d))
    peers.append((other_y, partner, d))
    for peer in peers:
        pl.semaphore_signal(barrier, inc=1, device_id=peer, device_id_type=MESH)
    pl.semaphore_wait(barrier, len(peers))

    @pl.when(is_inner)
    def _():
        for args in across:
            send_train(*args).start()

    @pl.when(jnp.logical_not(is_inner))
    def _():
        for args in across[:wide]:
            send_train(*args).start()

    load_q.wait()

    def largest(c, most):
        return jnp.maximum(most, jnp.max(jnp.abs(qf[:, cols(c)]), axis=1, keepdims=True))

    top = jnp.maximum(lax.fori_loop(0, chunks, largest, jnp.zeros((rows, 1), jnp.float32)), 1e-30)
    scales[z] = jnp.broadcast_to(top * (1.0 / (FULL * FULL)), (rows, 128))
    inverse = 1.0 / top

    def encode(c):
        x = qf[:, cols(c)]
        size = (jnp.sqrt(jnp.abs(x) * inverse) * FULL + 0.5).astype(jnp.int32)
        code[z, :, cols(c)] = jnp.where(x < 0, -size, size).astype(jnp.int16)

    def encode_wide(c, carry):
        encode(c)
        send_code(z, c, partner, own_send.at[0, c]).start()

        @pl.when(is_inner)
        def _():
            send_code(z, c, far_inner, own_send.at[1, c]).start()
        return carry

    lax.fori_loop(0, wide, encode_wide, 0)

    def send_scale(step):
        return remote(
            scales.at[z], scales.at[z], scale_send.at[step - 1], scale_recv.at[z],
            (y, lax.rem(z + step, steps), d))

    for step in range(1, steps):
        send_scale(step).start()

    def encode_rest(c, carry):
        encode(c)

        @pl.when(jnp.logical_not(is_inner))
        def _():
            send_code(z, c, partner, own_send.at[0, c]).start()
        return carry

    lax.fori_loop(wide, chunks, encode_rest, 0)

    def pick(table, ids):
        at = lax.broadcasted_iota(jnp.int32, (ids.shape[0], table.shape[1]), 1)
        return jnp.sum(jnp.where(at == ids, table, 0.0), axis=1, keepdims=True)

    def column(ids):
        count = ids.shape[1]
        square = (count, count)
        same = lax.broadcasted_iota(jnp.int32, square, 0) == lax.broadcasted_iota(jnp.int32, square, 1)
        wide_ids = jnp.broadcast_to(ids.astype(jnp.float32), square)
        return jnp.sum(jnp.where(same, wide_ids, 0.0), axis=1, keepdims=True).astype(jnp.int32)

    span = steps * rows
    train_scale = pick(tn_ref[...], column(eid_ref[...]))
    lane = lax.broadcasted_iota(jnp.int32, (rows, span), 1)
    own_lane = lax.rem(lane, rows) == lax.broadcasted_iota(jnp.int32, (rows, span), 0)
    train_row = jnp.sum(jnp.where(own_lane, train_scale, 0.0), axis=0, keepdims=True)
    query_scale = pick(qn_ref[...], column(qid_ref[...]))

    acc[...] = jnp.zeros_like(acc)
    load_t.wait()

    def multiply(c, held):
        coded = code[:, :, cols(c)].reshape(steps * rows, width).astype(jnp.int32).astype(jnp.float32)
        value = coded * jnp.abs(coded)
        upper = value.astype(jnp.bfloat16)
        lower = (value - upper.astype(jnp.float32)).astype(jnp.bfloat16)
        acc[:, :held] += lax.dot_general(
            jnp.concatenate([upper, lower], axis=0), tb[:held, cols(c)],
            (((1,), (1,)), ((), ())), preferred_element_type=jnp.float32,
        )

    narrow = groups * rows

    @pl.when(jnp.logical_not(is_inner))
    def _():
        for args in straight[wide:] + diagonal[wide:]:
            send_train(*args).start()

        def visit(c, carry):
            got_code(partner, c)
            got_code(far_inner, c)
            got_code(far_end, c)
            got_train(other_y, c)
            multiply(c, narrow)
            return carry

        lax.fori_loop(0, wide, visit, 0)

        def sent(c, carry):
            send_code(z, c, partner, own_send.at[0, c]).wait_send()
            return carry

        lax.fori_loop(0, chunks, sent, 0)
        for args in across[:wide] + straight[wide:] + diagonal[wide:]:
            send_train(*args).wait_send()

    @pl.when(is_inner)
    def _():
        def pass_on(c, carry):
            got_code(end, c)
            send_code(end, c, far_inner, fwd_send.at[0, c]).start()
            got_code(far_inner, c)
            send_code(far_inner, c, end, fwd_send.at[1, c]).start()
            return carry

        lax.fori_loop(0, wide, pass_on, 0)

        def rest(c, carry):
            send_code(z, c, far_inner, own_send.at[1, c]).start()
            return carry

        lax.fori_loop(wide, chunks, rest, 0)

        def visit(c, carry):
            got_code(far_end, c)
            send_code(far_end, c, end, fwd_send.at[2, c]).start()

            @pl.when(c < chunks - wide)
            def _():
                got_code(end, wide + c)
                send_code(end, wide + c, far_inner, fwd_send.at[0, wide + c]).start()

            got_train(other_y, c)
            multiply(c, narrow)
            return carry

        lax.fori_loop(0, wide, visit, 0)

        def close(c, carry):
            got_code(far_inner, c)
            got_code(far_end, c)
            got_train(other_y, c)
            got_train(2 + y, c)
            got_train(2 + other_y, c)
            multiply(c, 2 * narrow)
            return carry

        lax.fori_loop(wide, chunks, close, 0)

        def sent(c, carry):
            send_code(z, c, far_inner, own_send.at[1, c]).wait_send()
            send_code(end, c, far_inner, fwd_send.at[0, c]).wait_send()
            return carry

        lax.fori_loop(0, chunks, sent, 0)

        def sent_wide(c, carry):
            send_code(z, c, end, own_send.at[0, c]).wait_send()
            send_code(far_inner, c, end, fwd_send.at[1, c]).wait_send()
            send_code(far_end, c, end, fwd_send.at[2, c]).wait_send()
            return carry

        lax.fori_loop(0, wide, sent_wide, 0)
        for args in across:
            send_train(*args).wait_send()

    for step in range(1, steps):
        send_scale(step).wait_send()
        source = lax.rem(z + step, steps)
        remote(scales.at[source], scales.at[source], scale_send.at[0], scale_recv.at[source],
               (y, source, d)).wait_recv()

    lane_block = lane // rows
    for b in range(steps):
        at = pl.ds(b * rows, rows)
        product = (acc[at, :] + acc[pl.ds((steps + b) * rows, rows), :]) * scales[b][:, :1]
        near_at = lane_block == lax.rem(b - z + steps, steps)
        end_at = lane_block == lax.rem(b - end + steps, steps)
        for g in range(groups):
            near = jnp.concatenate([product[:, g * rows:(g + 1) * rows]] * steps, axis=1)
            far = jnp.concatenate([product[:, narrow + g * rows:narrow + (g + 1) * rows]] * steps, axis=1)
            block = jnp.where(near_at, near, 0.0) + jnp.where(end_at, far, 0.0)
            for to in range(dims):
                part[g * dims + to, pl.ds(b * mine, mine), :span] = block[to * mine:(to + 1) * mine]

    def send_part(step):
        at = lax.rem(place + step, plane)
        return remote(part.at[at], part_in.at[place], part_send.at[step - 1], part_recv.at[place],
                      (at // dims, z, lax.rem(at, dims)))

    def got_part(step):
        at = lax.rem(place + step, plane)
        remote(part.at[at], part_in.at[at], part_send.at[step - 1], part_recv.at[at],
               (at // dims, z, lax.rem(at, dims))).wait_recv()

    for step in range(1, plane):
        send_part(step).start()
    total = part[place]
    for step in range(1, plane):
        got_part(step)
        total = total + part_in[lax.rem(place + step, plane)]

    for b in range(steps):
        final[b, :mine, :] = total[b * mine:(b + 1) * mine]
        first = lane_block[:1] == lax.rem(b - z + steps, steps)
        final[b, mine:mine + 1, :span] = jnp.where(first, train_row, 0.0)

    def send_final(step):
        at = lax.rem(z + step, steps)
        return remote(final.at[at], final_in.at[z], final_send.at[step - 1], final_recv.at[z], (y, at, d))

    def got_final(step):
        at = lax.rem(z + step, steps)
        remote(final.at[at], final_in.at[at], final_send.at[step - 1], final_recv.at[at],
               (y, at, d)).wait_recv()

    for step in range(1, steps):
        send_final(step).start()
    summed = final[z]
    for step in range(1, steps):
        got_final(step)
        summed = summed + final_in[lax.rem(z + step, steps)]
    out_ref[...] = summed[:mine, :span] / (query_scale * summed[mine:mine + 1, :span])

    for step in range(1, plane):
        send_part(step).wait_send()
    for step in range(1, steps):
        send_final(step).wait_send()


def all_pairs(sizes, query_grads, train_grads, example_ids, query_ids, query_norms, train_norms):
    groups, steps, dims = sizes
    rows, depth = query_grads.shape
    half = depth // groups
    width = min(WIDTH, half // 8)
    chunks = half // width
    wide = (chunks * 5) // 8
    plane = groups * dims
    dma, vmem = pltpu.SemaphoreType.DMA, pltpu.VMEM
    whole = pl.BlockSpec(memory_space=pltpu.VMEM)
    anywhere = pl.BlockSpec(memory_space=pl.ANY)
    return pl.pallas_call(
        functools.partial(kernel, sizes, width, wide),
        out_shape=jax.ShapeDtypeStruct((rows // dims, steps * rows), jnp.float32),
        in_specs=[anywhere, anywhere, whole, whole, whole, whole],
        out_specs=whole,
        scratch_shapes=[
            vmem((rows, half), jnp.float32),
            vmem((steps, rows, half), jnp.int16),
            vmem((2 * groups * rows, half), jnp.bfloat16),
            vmem((2 * steps * rows, 2 * groups * rows), jnp.float32),
            vmem((steps, rows, 128), jnp.float32),
            vmem((plane, rows, 128), jnp.float32),
            vmem((plane, rows, 128), jnp.float32),
            vmem((steps, 8, 128), jnp.float32),
            vmem((steps, 8, 128), jnp.float32),
            dma((2,)),
            dma((2, chunks)),
            dma((3, chunks)),
            dma((steps, chunks)),
            dma((2, chunks)),
            dma((2 * groups, chunks)),
            dma((steps - 1,)),
            dma((steps,)),
            dma((plane - 1,)),
            dma((plane,)),
            dma((steps - 1,)),
            dma((steps,)),
        ],
        compiler_params=pltpu.CompilerParams(
            collective_id=0, has_side_effects=True, vmem_limit_bytes=32 * 1024 * 1024),
    )(
        query_grads, train_grads, example_ids.reshape(1, -1), query_ids.reshape(1, -1),
        query_norms.reshape(1, -1), train_norms.reshape(1, -1),
    )


def solution(mesh):
    in_specs = (
        P("query", "dim"),
        P(("groups", "query"), "dim"),
        P(("groups", "query")),
        P(("query", "dim")),
        P(),
        P("groups"),
    )
    out_specs = P(("groups", "query", "dim"), None)
    sizes = tuple(mesh.shape[axis] for axis in ("groups", "query", "dim"))
    body = functools.partial(all_pairs, sizes) if sizes[:2] == (2, STEPS) else on_device
    return jax.shard_map(
        body, mesh=mesh, in_specs=in_specs, out_specs=out_specs, check_vma=False
    )
```

```python
import functools

import jax
import jax.numpy as jnp
from jax import lax
from jax.experimental import pallas as pl
from jax.experimental.pallas import tpu as pltpu
from jax.sharding import PartitionSpec as P

STEPS = 4
WIDTH = 4096
FULL = 32767.0
MESH = pl.DeviceIdType.MESH


def passed_along(value, axis, by):
    size = lax.axis_size(axis)
    return lax.ppermute(value, axis, [(i, (i + by) % size) for i in range(size)])


def partial_scores(queries, span):
    return lax.dot_general(
        queries,
        span.astype(jnp.float32),
        (((1,), (1,)), ((), ())),
        precision=lax.Precision.HIGHEST,
        preferred_element_type=jnp.float32,
    )


def lookup(table, indices):
    matches = indices[:, None] == lax.iota(jnp.int32, table.shape[0])[None, :]
    return jnp.sum(jnp.where(matches, table[None, :], 0.0), axis=1)


def on_device(query_grads, train_grads, example_ids, query_ids, query_norms, train_norms):
    visited = [(train_grads, example_ids)]
    current = train_grads
    current_ids = example_ids
    for offset in range(1, STEPS):
        current, current_ids = passed_along((current, current_ids), "query", 1)
        visited.append((current, current_ids))
    partials = [partial_scores(query_grads, span) for span, span_ids in visited]
    summed = jnp.concatenate(
        [lax.psum_scatter(piece, "dim", scatter_dimension=0, tiled=True) for piece in partials],
        axis=1,
    )
    seen_ids = jnp.concatenate([span_ids for span, span_ids in visited], axis=0)
    train_scale = lookup(train_norms, seen_ids)
    query_scale = lookup(query_norms, query_ids)
    return summed / (query_scale[:, None] * train_scale[None, :])


def kernel(
    sizes, width, wide,
    q_ref, t_ref, eid_hbm, qid_hbm, qn_hbm, tn_hbm, out_ref,
    qf, eid_ref, qid_ref, qn_ref, tn_ref, code, tb, acc, scales, tiles, tiles_in,
    local_sem, own_send, fwd_send, q_recv, t_send, t_recv,
    scale_send, scale_recv, tile_send, tile_recv,
):
    groups, steps, dims = sizes
    rows = q_ref.shape[0]
    mine = rows // dims
    half = qf.shape[1]
    chunks = half // width
    y, z, d = lax.axis_index("groups"), lax.axis_index("query"), lax.axis_index("dim")
    other_y = 1 - y
    high = z // 2
    is_inner = jnp.logical_or(z == 1, z == 2)
    partner = jnp.where(high == 0, 1 - z, 5 - z)
    end = jnp.where(high == 0, 0, 3)
    far_inner = jnp.where(high == 0, 2, 1)
    far_end = jnp.where(high == 0, 3, 0)
    plane = groups * dims
    in_plane = y * dims + d

    def cols(c, base=0):
        return pl.ds(pl.multiple_of(base + c * width, width), width)

    def remote(src, dst, send, recv, to):
        return pltpu.make_async_remote_copy(
            src_ref=src, dst_ref=dst, send_sem=send, recv_sem=recv,
            device_id=to, device_id_type=MESH,
        )

    def send_code(block, c, to_z, send):
        view = code.at[block, :, cols(c)]
        return remote(view, view, send, q_recv.at[block, c], (y, to_z, d))

    def got_code(block, c):
        send_code(block, c, partner, own_send.at[0, c]).wait_recv()

    def send_train(c, half_of, slot, send, to):
        return remote(
            t_ref.at[:, cols(c, half_of * half)],
            tb.at[pl.ds(pl.multiple_of(slot * rows, rows), rows), cols(c)],
            send, t_recv.at[slot, c], to,
        )

    def got_train(slot, c):
        send_train(c, y, slot, t_send.at[0, c], (y, partner, d)).wait_recv()

    across = [(c, other_y, y, t_send.at[0, c], (other_y, z, d)) for c in range(chunks)]
    diagonal = [(c, other_y, 2 + y, t_send.at[0, c], (other_y, partner, d)) for c in range(chunks)]
    straight = [(c, y, 2 + y, t_send.at[1, c], (y, partner, d)) for c in range(chunks)]

    load_q = pltpu.make_async_copy(
        q_ref.at[:, pl.ds(pl.multiple_of(y * half, half), half)], qf, local_sem.at[0])
    load_t = pltpu.make_async_copy(
        t_ref.at[:, pl.ds(pl.multiple_of(y * half, half), half)],
        tb.at[pl.ds(pl.multiple_of(y * rows, rows), rows), :], local_sem.at[1])
    load_q.start()
    load_t.start()
    tables = [
        pltpu.make_async_copy(src, dst, local_sem.at[2 + at])
        for at, (src, dst) in enumerate(
            [(eid_hbm, eid_ref), (qid_hbm, qid_ref), (qn_hbm, qn_ref), (tn_hbm, tn_ref)])
    ]
    for table in tables:
        table.start()

    barrier = pltpu.get_barrier_semaphore()
    peers = []
    for step in range(1, plane):
        at = lax.rem(in_plane + step, plane)
        peers.append((at // dims, z, lax.rem(at, dims)))
    for step in range(1, steps):
        peers.append((y, lax.rem(z + step, steps), d))
    peers.append((other_y, partner, d))
    for peer in peers:
        pl.semaphore_signal(barrier, inc=1, device_id=peer, device_id_type=MESH)
    pl.semaphore_wait(barrier, len(peers))

    @pl.when(is_inner)
    def _():
        for args in across:
            send_train(*args).start()

    @pl.when(jnp.logical_not(is_inner))
    def _():
        for args in across[:wide]:
            send_train(*args).start()

    load_q.wait()

    def largest(c, most):
        return jnp.maximum(most, jnp.max(jnp.abs(qf[:, cols(c)]), axis=1, keepdims=True))

    top = jnp.maximum(lax.fori_loop(0, chunks, largest, jnp.zeros((rows, 1), jnp.float32)), 1e-30)
    scales[z] = jnp.broadcast_to(top * (1.0 / (FULL * FULL)), (rows, 128))
    inverse = 1.0 / top

    def encode(c):
        x = qf[:, cols(c)]
        size = (jnp.sqrt(jnp.abs(x) * inverse) * FULL + 0.5).astype(jnp.int32)
        code[z, :, cols(c)] = jnp.where(x < 0, -size, size).astype(jnp.int16)

    def encode_wide(c, carry):
        encode(c)
        send_code(z, c, partner, own_send.at[0, c]).start()

        @pl.when(is_inner)
        def _():
            send_code(z, c, far_inner, own_send.at[1, c]).start()
        return carry

    lax.fori_loop(0, wide, encode_wide, 0)

    def send_scale(step):
        return remote(
            scales.at[z], scales.at[z], scale_send.at[step - 1], scale_recv.at[z],
            (y, lax.rem(z + step, steps), d))

    for step in range(1, steps):
        send_scale(step).start()

    def encode_rest(c, carry):
        encode(c)

        @pl.when(jnp.logical_not(is_inner))
        def _():
            send_code(z, c, partner, own_send.at[0, c]).start()
        return carry

    lax.fori_loop(wide, chunks, encode_rest, 0)

    def pick(table, ids):
        at = lax.broadcasted_iota(jnp.int32, (ids.shape[0], table.shape[1]), 1)
        return jnp.sum(jnp.where(at == ids, table, 0.0), axis=1, keepdims=True)

    def column(ids):
        count = ids.shape[1]
        square = (count, count)
        same = lax.broadcasted_iota(jnp.int32, square, 0) == lax.broadcasted_iota(jnp.int32, square, 1)
        wide_ids = jnp.broadcast_to(ids.astype(jnp.float32), square)
        return jnp.sum(jnp.where(same, wide_ids, 0.0), axis=1, keepdims=True).astype(jnp.int32)

    for table in tables:
        table.wait()
    train_scale = pick(tn_ref[...], column(eid_ref[...]))
    span = steps * rows
    lane = lax.broadcasted_iota(jnp.int32, (rows, 128), 1)
    own_lane = lane == lax.broadcasted_iota(jnp.int32, (rows, 128), 0) + 2 * groups * rows
    train_row = jnp.sum(jnp.where(own_lane, train_scale, 0.0), axis=0, keepdims=True)
    query_scale = pick(qn_ref[...], column(qid_ref[...]))

    acc[...] = jnp.zeros_like(acc)
    load_t.wait()

    def multiply(c, held):
        coded = code[:, :, cols(c)].reshape(steps * rows, width).astype(jnp.int32).astype(jnp.float32)
        value = coded * jnp.abs(coded)
        upper = value.astype(jnp.bfloat16)
        lower = (value - upper.astype(jnp.float32)).astype(jnp.bfloat16)
        acc[:, :held] += lax.dot_general(
            jnp.concatenate([upper, lower], axis=0), tb[:held, cols(c)],
            (((1,), (1,)), ((), ())), preferred_element_type=jnp.float32,
        )

    narrow = groups * rows

    around = [
        [lax.rem(at + step, size) for step in range(size)]
        for at, size in zip((y, z, d), sizes)
    ]
    peers_all = [
        (to_y, to_z, to_d)
        for at_z, to_z in enumerate(around[1])
        for at_y, to_y in enumerate(around[0])
        for at_d, to_d in enumerate(around[2])
        if at_y + at_z + at_d
    ]

    def slot(peer):
        return (peer[0] * steps + peer[1]) * dims + peer[2]

    place = slot((y, z, d))

    def send_tile(at):
        peer = peers_all[at]
        return remote(tiles.at[peer[1] * dims + peer[2]], tiles_in.at[place],
                      tile_send.at[at], tile_recv.at[place], peer)

    def got_tile(at):
        peer = peers_all[at]
        remote(tiles.at[peer[1] * dims + peer[2]], tiles_in.at[slot(peer)],
               tile_send.at[at], tile_recv.at[slot(peer)], peer).wait_recv()

    def give_tiles():
        for step in range(1, steps):
            source = lax.rem(z + step, steps)
            remote(scales.at[source], scales.at[source], scale_send.at[0], scale_recv.at[source],
                   (y, source, d)).wait_recv()
        for b in range(steps):
            pieces = acc[pl.ds(b * rows, rows), :] + acc[pl.ds((steps + b) * rows, rows), :]
            product = pieces * scales[b] + train_row
            for to in range(dims):
                tiles[b * dims + to] = product[to * mine:(to + 1) * mine]
        for at in range(len(peers_all)):
            send_tile(at).start()
        tiles_in[place] = tiles[z * dims + d]

    @pl.when(jnp.logical_not(is_inner))
    def _():
        for args in straight[wide:] + diagonal[wide:]:
            send_train(*args).start()

        def visit(c, carry):
            got_code(partner, c)
            got_code(far_inner, c)
            got_code(far_end, c)
            got_train(other_y, c)
            multiply(c, narrow)
            return carry

        lax.fori_loop(0, wide, visit, 0)
        give_tiles()

    @pl.when(is_inner)
    def _():
        def pass_on(c, carry):
            got_code(end, c)
            send_code(end, c, far_inner, fwd_send.at[0, c]).start()
            got_code(far_inner, c)
            send_code(far_inner, c, end, fwd_send.at[1, c]).start()
            return carry

        lax.fori_loop(0, wide, pass_on, 0)

        def rest(c, carry):
            send_code(z, c, far_inner, own_send.at[1, c]).start()
            return carry

        lax.fori_loop(wide, chunks, rest, 0)

        def visit(c, carry):
            got_code(far_end, c)
            send_code(far_end, c, end, fwd_send.at[2, c]).start()

            @pl.when(c < chunks - wide)
            def _():
                got_code(end, wide + c)
                send_code(end, wide + c, far_inner, fwd_send.at[0, wide + c]).start()

            got_train(other_y, c)
            multiply(c, narrow)
            return carry

        lax.fori_loop(0, wide, visit, 0)

        def close(c, carry):
            got_code(far_inner, c)
            got_code(far_end, c)
            got_train(other_y, c)
            got_train(2 + y, c)
            got_train(2 + other_y, c)
            multiply(c, 2 * narrow)
            return carry

        lax.fori_loop(wide, chunks, close, 0)
        give_tiles()

    for at in range(len(peers_all)):
        got_tile(at)
    by_source = tiles_in[...].reshape(groups, steps, dims, mine, 128)
    summed = jnp.sum(jnp.sum(by_source, axis=2), axis=0)

    def lanes_of(block, role):
        first = [(role * groups + g) * rows for g in range(groups)]
        return jnp.where(y == 0, block[:, first[0]:first[0] + rows], block[:, first[1]:first[1] + rows])

    raw = [lanes_of(summed[k], 0) for k in range(steps)]
    raw[0] = raw[0] + lanes_of(summed[1], 1)
    raw[3] = raw[3] + lanes_of(summed[2], 1)
    lane_block = lax.broadcasted_iota(jnp.int32, (mine, span), 1) // rows
    scores = jnp.zeros((mine, span), jnp.float32)
    for k in range(steps):
        train = tiles_in[slot((y, k, d))][:, 2 * groups * rows:2 * groups * rows + rows]
        value = raw[k] / (query_scale * train)
        here = lane_block == lax.rem(z - k + steps, steps)
        scores = scores + jnp.where(here, jnp.concatenate([value] * steps, axis=1), 0.0)
    out_ref[...] = scores

    @pl.when(jnp.logical_not(is_inner))
    def _():
        def sent(c, carry):
            send_code(z, c, partner, own_send.at[0, c]).wait_send()
            return carry

        lax.fori_loop(0, chunks, sent, 0)
        for args in across[:wide] + straight[wide:] + diagonal[wide:]:
            send_train(*args).wait_send()

    @pl.when(is_inner)
    def _():
        def sent(c, carry):
            send_code(z, c, far_inner, own_send.at[1, c]).wait_send()
            send_code(end, c, far_inner, fwd_send.at[0, c]).wait_send()
            return carry

        lax.fori_loop(0, chunks, sent, 0)

        def sent_wide(c, carry):
            send_code(z, c, end, own_send.at[0, c]).wait_send()
            send_code(far_inner, c, end, fwd_send.at[1, c]).wait_send()
            send_code(far_end, c, end, fwd_send.at[2, c]).wait_send()
            return carry

        lax.fori_loop(0, wide, sent_wide, 0)
        for args in across:
            send_train(*args).wait_send()

    for step in range(1, steps):
        send_scale(step).wait_send()
    for at in range(len(peers_all)):
        send_tile(at).wait_send()


def all_pairs(sizes, query_grads, train_grads, example_ids, query_ids, query_norms, train_norms):
    groups, steps, dims = sizes
    rows, depth = query_grads.shape
    half = depth // groups
    width = min(WIDTH, half // 8)
    chunks = half // width
    wide = (chunks * 5) // 8
    plane = groups * dims
    dma, vmem = pltpu.SemaphoreType.DMA, pltpu.VMEM
    whole = pl.BlockSpec(memory_space=pltpu.VMEM)
    in_hbm = pl.BlockSpec(memory_space=pltpu.HBM)
    return pl.pallas_call(
        functools.partial(kernel, sizes, width, wide),
        out_shape=jax.ShapeDtypeStruct((rows // dims, steps * rows), jnp.float32),
        in_specs=[in_hbm] * 6,
        out_specs=whole,
        scratch_shapes=[
            vmem((rows, half), jnp.float32),
            vmem((1, example_ids.shape[0]), jnp.int32),
            vmem((1, query_ids.shape[0]), jnp.int32),
            vmem((1, query_norms.shape[0]), jnp.float32),
            vmem((1, train_norms.shape[0]), jnp.float32),
            vmem((steps, rows, half), jnp.int16),
            vmem((2 * groups * rows, half), jnp.bfloat16),
            vmem((2 * steps * rows, 128), jnp.float32),
            vmem((steps, rows, 128), jnp.float32),
            vmem((steps * dims, rows // dims, 128), jnp.float32),
            vmem((steps * plane, rows // dims, 128), jnp.float32),
            dma((6,)),
            dma((2, chunks)),
            dma((3, chunks)),
            dma((steps, chunks)),
            dma((2, chunks)),
            dma((2 * groups, chunks)),
            dma((steps - 1,)),
            dma((steps,)),
            dma((steps * plane - 1,)),
            dma((steps * plane,)),
        ],
        compiler_params=pltpu.CompilerParams(
            collective_id=0, has_side_effects=True, vmem_limit_bytes=60 * 1024 * 1024),
    )(
        query_grads, train_grads, example_ids.reshape(1, -1), query_ids.reshape(1, -1),
        query_norms.reshape(1, -1), train_norms.reshape(1, -1),
    )


def solution(mesh):
    in_specs = (
        P("query", "dim"),
        P(("groups", "query"), "dim"),
        P(("groups", "query")),
        P(("query", "dim")),
        P(),
        P("groups"),
    )
    out_specs = P(("groups", "query", "dim"), None)
    sizes = tuple(mesh.shape[axis] for axis in ("groups", "query", "dim"))
    body = functools.partial(all_pairs, sizes) if sizes[:2] == (2, STEPS) else on_device
    return jax.shard_map(
        body, mesh=mesh, in_specs=in_specs, out_specs=out_specs, check_vma=False
    )
```

```python
import functools

import jax
import jax.numpy as jnp
from jax import lax
from jax.experimental import pallas as pl
from jax.experimental.pallas import tpu as pltpu
from jax.sharding import PartitionSpec as P

STEPS = 4
WIDTH = 4096
FULL = 32767.0
MESH = pl.DeviceIdType.MESH


def passed_along(value, axis, by):
    size = lax.axis_size(axis)
    return lax.ppermute(value, axis, [(i, (i + by) % size) for i in range(size)])


def partial_scores(queries, span):
    return lax.dot_general(
        queries,
        span.astype(jnp.float32),
        (((1,), (1,)), ((), ())),
        precision=lax.Precision.HIGHEST,
        preferred_element_type=jnp.float32,
    )


def lookup(table, indices):
    matches = indices[:, None] == lax.iota(jnp.int32, table.shape[0])[None, :]
    return jnp.sum(jnp.where(matches, table[None, :], 0.0), axis=1)


def on_device(query_grads, train_grads, example_ids, query_ids, query_norms, train_norms):
    visited = [(train_grads, example_ids)]
    current = train_grads
    current_ids = example_ids
    for offset in range(1, STEPS):
        current, current_ids = passed_along((current, current_ids), "query", 1)
        visited.append((current, current_ids))
    partials = [partial_scores(query_grads, span) for span, span_ids in visited]
    summed = jnp.concatenate(
        [lax.psum_scatter(piece, "dim", scatter_dimension=0, tiled=True) for piece in partials],
        axis=1,
    )
    seen_ids = jnp.concatenate([span_ids for span, span_ids in visited], axis=0)
    train_scale = lookup(train_norms, seen_ids)
    query_scale = lookup(query_norms, query_ids)
    return summed / (query_scale[:, None] * train_scale[None, :])


def kernel(
    sizes, width, wide,
    q_ref, t_ref, eid_hbm, qid_hbm, qn_hbm, tn_hbm, out_ref,
    qf, eid_ref, qid_ref, qn_ref, tn_ref, code, tb, acc, scales, tiles, tiles_in,
    local_sem, own_send, fwd_send, q_recv, t_send, t_recv,
    scale_send, scale_recv, tile_send, tile_recv,
):
    groups, steps, dims = sizes
    rows = q_ref.shape[0]
    mine = rows // dims
    half = qf.shape[1]
    chunks = half // width
    y, z, d = lax.axis_index("groups"), lax.axis_index("query"), lax.axis_index("dim")
    other_y = 1 - y
    high = z // 2
    is_inner = jnp.logical_or(z == 1, z == 2)
    partner = jnp.where(high == 0, 1 - z, 5 - z)
    end = jnp.where(high == 0, 0, 3)
    far_inner = jnp.where(high == 0, 2, 1)
    far_end = jnp.where(high == 0, 3, 0)
    plane = groups * dims
    in_plane = y * dims + d

    def cols(c, base=0):
        return pl.ds(pl.multiple_of(base + c * width, width), width)

    def remote(src, dst, send, recv, to):
        return pltpu.make_async_remote_copy(
            src_ref=src, dst_ref=dst, send_sem=send, recv_sem=recv,
            device_id=to, device_id_type=MESH,
        )

    def send_code(block, c, to_z, send):
        view = code.at[block, :, cols(c)]
        return remote(view, view, send, q_recv.at[block, c], (y, to_z, d))

    def got_code(block, c):
        send_code(block, c, partner, own_send.at[0, c]).wait_recv()

    def send_train(c, half_of, slot, send, to):
        return remote(
            t_ref.at[:, cols(c, half_of * half)],
            tb.at[pl.ds(pl.multiple_of(slot * rows, rows), rows), cols(c)],
            send, t_recv.at[slot, c], to,
        )

    def got_train(slot, c):
        send_train(c, y, slot, t_send.at[0, c], (y, partner, d)).wait_recv()

    across = [(c, other_y, y, t_send.at[0, c], (other_y, z, d)) for c in range(chunks)]
    diagonal = [(c, other_y, 2 + y, t_send.at[0, c], (other_y, partner, d)) for c in range(chunks)]
    straight = [(c, y, 2 + y, t_send.at[1, c], (y, partner, d)) for c in range(chunks)]

    load_q = pltpu.make_async_copy(
        q_ref.at[:, pl.ds(pl.multiple_of(y * half, half), half)], qf, local_sem.at[0])
    load_t = pltpu.make_async_copy(
        t_ref.at[:, pl.ds(pl.multiple_of(y * half, half), half)],
        tb.at[pl.ds(pl.multiple_of(y * rows, rows), rows), :], local_sem.at[1])
    load_q.start()
    load_t.start()
    tables = [
        pltpu.make_async_copy(src, dst, local_sem.at[2 + at])
        for at, (src, dst) in enumerate(
            [(eid_hbm, eid_ref), (qid_hbm, qid_ref), (qn_hbm, qn_ref), (tn_hbm, tn_ref)])
    ]
    for table in tables:
        table.start()

    barrier = pltpu.get_barrier_semaphore()
    peers = []
    for step in range(1, plane):
        at = lax.rem(in_plane + step, plane)
        peers.append((at // dims, z, lax.rem(at, dims)))
    for step in range(1, steps):
        peers.append((y, lax.rem(z + step, steps), d))
    peers.append((other_y, partner, d))
    for peer in peers:
        pl.semaphore_signal(barrier, inc=1, device_id=peer, device_id_type=MESH)
    load_q.wait()

    def largest(c, most):
        return jnp.maximum(most, jnp.max(jnp.abs(qf[:, cols(c)]), axis=1, keepdims=True))

    top = jnp.maximum(lax.fori_loop(0, chunks, largest, jnp.zeros((rows, 1), jnp.float32)), 1e-30)
    scales[z] = jnp.broadcast_to(top * (1.0 / (FULL * FULL)), (rows, 128))
    inverse = 1.0 / top

    def encode(c):
        x = qf[:, cols(c)]
        size = (jnp.sqrt(jnp.abs(x) * inverse) * FULL + 0.5).astype(jnp.int32)
        code[z, :, cols(c)] = jnp.where(x < 0, -size, size).astype(jnp.int16)

    def send_wide(c):
        @pl.when(is_inner)
        def _():
            send_code(z, c, far_inner, own_send.at[1, c]).start()

        send_code(z, c, partner, own_send.at[0, c]).start()

    def encode_wide(c, carry):
        encode(c)
        send_wide(c)
        return carry

    encode(0)
    pl.semaphore_wait(barrier, len(peers))
    send_wide(0)
    lax.fori_loop(1, wide, encode_wide, 0)

    @pl.when(is_inner)
    def _():
        for args in across:
            send_train(*args).start()

    @pl.when(jnp.logical_not(is_inner))
    def _():
        for args in across[:wide]:
            send_train(*args).start()

    def send_scale(step):
        return remote(
            scales.at[z], scales.at[z], scale_send.at[step - 1], scale_recv.at[z],
            (y, lax.rem(z + step, steps), d))

    for step in range(1, steps):
        send_scale(step).start()

    def encode_rest(c, carry):
        encode(c)

        @pl.when(jnp.logical_not(is_inner))
        def _():
            send_code(z, c, partner, own_send.at[0, c]).start()
        return carry

    lax.fori_loop(wide, chunks, encode_rest, 0)

    def pick(table, ids):
        at = lax.broadcasted_iota(jnp.int32, (ids.shape[0], table.shape[1]), 1)
        return jnp.sum(jnp.where(at == ids, table, 0.0), axis=1, keepdims=True)

    def column(ids):
        count = ids.shape[1]
        square = (count, count)
        same = lax.broadcasted_iota(jnp.int32, square, 0) == lax.broadcasted_iota(jnp.int32, square, 1)
        wide_ids = jnp.broadcast_to(ids.astype(jnp.float32), square)
        return jnp.sum(jnp.where(same, wide_ids, 0.0), axis=1, keepdims=True).astype(jnp.int32)

    for table in tables:
        table.wait()
    train_scale = pick(tn_ref[...], column(eid_ref[...]))
    span = steps * rows
    lane = lax.broadcasted_iota(jnp.int32, (rows, 128), 1)
    own_lane = lane == lax.broadcasted_iota(jnp.int32, (rows, 128), 0) + 2 * groups * rows
    train_row = jnp.sum(jnp.where(own_lane, train_scale, 0.0), axis=0, keepdims=True)
    query_scale = pick(qn_ref[...], column(qid_ref[...]))

    acc[...] = jnp.zeros_like(acc)
    load_t.wait()

    def multiply(c, held):
        coded = code[:, :, cols(c)].reshape(steps * rows, width).astype(jnp.int32).astype(jnp.float32)
        value = coded * jnp.abs(coded)
        upper = value.astype(jnp.bfloat16)
        lower = (value - upper.astype(jnp.float32)).astype(jnp.bfloat16)
        acc[:, :held] += lax.dot_general(
            jnp.concatenate([upper, lower], axis=0), tb[:held, cols(c)],
            (((1,), (1,)), ((), ())), preferred_element_type=jnp.float32,
        )

    narrow = groups * rows

    around = [
        [lax.rem(at + step, size) for step in range(size)]
        for at, size in zip((y, z, d), sizes)
    ]
    peers_all = [
        (to_y, to_z, to_d)
        for at_z, to_z in enumerate(around[1])
        for at_y, to_y in enumerate(around[0])
        for at_d, to_d in enumerate(around[2])
        if at_y + at_z + at_d
    ]

    offsets_z = [
        at_z
        for at_z in range(steps)
        for at_y in range(groups)
        for at_d in range(dims)
        if at_y + at_z + at_d
    ]

    def slot(peer):
        return (peer[0] * steps + peer[1]) * dims + peer[2]

    place = slot((y, z, d))

    def send_tile(at):
        peer = peers_all[at]
        return remote(tiles.at[peer[1] * dims + peer[2]], tiles_in.at[place],
                      tile_send.at[0], tile_recv.at[0], peer)

    def give_tiles():
        for step in range(1, steps):
            source = lax.rem(z + step, steps)
            remote(scales.at[source], scales.at[source], scale_send.at[0], scale_recv.at[source],
                   (y, source, d)).wait_recv()
        for at_z in (2, 1, 3, 0):
            to_z = around[1][at_z]
            upper = acc[pl.ds(pl.multiple_of(to_z * rows, rows), rows), :]
            lower = acc[pl.ds(pl.multiple_of((steps + to_z) * rows, rows), rows), :]
            product = (upper + lower) * scales[to_z] + train_row
            for to in range(dims):
                tiles[to_z * dims + to] = product[to * mine:(to + 1) * mine]
            for at, peer_z in enumerate(offsets_z):
                if peer_z == at_z:
                    send_tile(at).start()
        tiles_in[place] = tiles[z * dims + d]

    @pl.when(jnp.logical_not(is_inner))
    def _():
        for args in straight[wide:] + diagonal[wide:]:
            send_train(*args).start()

        def visit(c, carry):
            got_code(partner, c)
            got_code(far_inner, c)
            got_code(far_end, c)
            got_train(other_y, c)
            multiply(c, narrow)
            return carry

        lax.fori_loop(0, wide, visit, 0)
        give_tiles()

        def sent(c, carry):
            send_code(z, c, partner, own_send.at[0, c]).wait_send()
            return carry

        lax.fori_loop(0, chunks, sent, 0)
        for args in across[:wide] + straight[wide:] + diagonal[wide:]:
            send_train(*args).wait_send()

    @pl.when(is_inner)
    def _():
        def pass_on(c, carry):
            got_code(end, c)
            send_code(end, c, far_inner, fwd_send.at[0, c]).start()
            got_code(far_inner, c)
            send_code(far_inner, c, end, fwd_send.at[1, c]).start()
            return carry

        lax.fori_loop(0, wide, pass_on, 0)

        def rest(c, carry):
            send_code(z, c, far_inner, own_send.at[1, c]).start()
            return carry

        lax.fori_loop(wide, chunks, rest, 0)

        def visit(c, carry):
            got_code(far_end, c)
            send_code(far_end, c, end, fwd_send.at[2, c]).start()

            @pl.when(c < chunks - wide)
            def _():
                got_code(end, wide + c)
                send_code(end, wide + c, far_inner, fwd_send.at[0, wide + c]).start()

            got_train(other_y, c)
            multiply(c, narrow)
            return carry

        lax.fori_loop(0, wide, visit, 0)

        def close(c, carry):
            got_code(far_inner, c)
            got_code(far_end, c)
            got_train(other_y, c)
            got_train(2 + y, c)
            got_train(2 + other_y, c)
            multiply(c, 2 * narrow)
            return carry

        lax.fori_loop(wide, chunks, close, 0)
        give_tiles()

        def sent(c, carry):
            send_code(z, c, far_inner, own_send.at[1, c]).wait_send()
            send_code(end, c, far_inner, fwd_send.at[0, c]).wait_send()
            return carry

        lax.fori_loop(0, chunks, sent, 0)

        def sent_wide(c, carry):
            send_code(z, c, end, own_send.at[0, c]).wait_send()
            send_code(far_inner, c, end, fwd_send.at[1, c]).wait_send()
            send_code(far_end, c, end, fwd_send.at[2, c]).wait_send()
            return carry

        lax.fori_loop(0, wide, sent_wide, 0)
        for args in across:
            send_train(*args).wait_send()

    for step in range(1, steps):
        send_scale(step).wait_send()
    others = tiles_in.at[pl.ds(0, len(peers_all))]
    all_tiles = remote(others, others, tile_send.at[0], tile_recv.at[0], peers_all[0])
    all_tiles.wait_recv()
    by_source = tiles_in[...].reshape(groups, steps, dims, mine, 128)
    summed = jnp.sum(jnp.sum(by_source, axis=2), axis=0)

    def lanes_of(block, role):
        first = [(role * groups + g) * rows for g in range(groups)]
        return jnp.where(y == 0, block[:, first[0]:first[0] + rows], block[:, first[1]:first[1] + rows])

    raw = [lanes_of(summed[k], 0) for k in range(steps)]
    raw[0] = raw[0] + lanes_of(summed[1], 1)
    raw[3] = raw[3] + lanes_of(summed[2], 1)
    lane_block = lax.broadcasted_iota(jnp.int32, (mine, span), 1) // rows
    scores = jnp.zeros((mine, span), jnp.float32)
    for k in range(steps):
        train = tiles_in[slot((y, k, d))][:, 2 * groups * rows:2 * groups * rows + rows]
        value = raw[k] / (query_scale * train)
        here = lane_block == lax.rem(z - k + steps, steps)
        scores = scores + jnp.where(here, jnp.concatenate([value] * steps, axis=1), 0.0)
    out_ref[...] = scores

    all_tiles.wait_send()


def all_pairs(sizes, query_grads, train_grads, example_ids, query_ids, query_norms, train_norms):
    groups, steps, dims = sizes
    rows, depth = query_grads.shape
    half = depth // groups
    width = min(WIDTH, half // 8)
    chunks = half // width
    wide = (chunks * 5) // 8
    plane = groups * dims
    dma, vmem = pltpu.SemaphoreType.DMA, pltpu.VMEM
    whole = pl.BlockSpec(memory_space=pltpu.VMEM)
    in_hbm = pl.BlockSpec(memory_space=pltpu.HBM)
    return pl.pallas_call(
        functools.partial(kernel, sizes, width, wide),
        out_shape=jax.ShapeDtypeStruct((rows // dims, steps * rows), jnp.float32),
        in_specs=[in_hbm] * 6,
        out_specs=whole,
        scratch_shapes=[
            vmem((rows, half), jnp.float32),
            vmem((1, example_ids.shape[0]), jnp.int32),
            vmem((1, query_ids.shape[0]), jnp.int32),
            vmem((1, query_norms.shape[0]), jnp.float32),
            vmem((1, train_norms.shape[0]), jnp.float32),
            vmem((steps, rows, half), jnp.int16),
            vmem((2 * groups * rows, half), jnp.bfloat16),
            vmem((2 * steps * rows, 128), jnp.float32),
            vmem((steps, rows, 128), jnp.float32),
            vmem((steps * dims, rows // dims, 128), jnp.float32),
            vmem((steps * plane, rows // dims, 128), jnp.float32),
            dma((6,)),
            dma((2, chunks)),
            dma((3, chunks)),
            dma((steps, chunks)),
            dma((2, chunks)),
            dma((2 * groups, chunks)),
            dma((steps - 1,)),
            dma((steps,)),
            dma((1,)),
            dma((1,)),
        ],
        compiler_params=pltpu.CompilerParams(
            collective_id=0, has_side_effects=True, vmem_limit_bytes=60 * 1024 * 1024),
    )(
        query_grads, train_grads, example_ids.reshape(1, -1), query_ids.reshape(1, -1),
        query_norms.reshape(1, -1), train_norms.reshape(1, -1),
    )


def solution(mesh):
    in_specs = (
        P("query", "dim"),
        P(("groups", "query"), "dim"),
        P(("groups", "query")),
        P(("query", "dim")),
        P(),
        P("groups"),
    )
    out_specs = P(("groups", "query", "dim"), None)
    sizes = tuple(mesh.shape[axis] for axis in ("groups", "query", "dim"))
    body = functools.partial(all_pairs, sizes) if sizes[:2] == (2, STEPS) else on_device
    return jax.shard_map(
        body, mesh=mesh, in_specs=in_specs, out_specs=out_specs, check_vma=False
    )
```

```python
import functools

import jax
import jax.numpy as jnp
from jax import lax
from jax.experimental import pallas as pl
from jax.experimental.pallas import tpu as pltpu
from jax.sharding import PartitionSpec as P

STEPS = 4
WIDTH = 4096
FULL = 32767.0
MESH = pl.DeviceIdType.MESH


def passed_along(value, axis, by):
    size = lax.axis_size(axis)
    return lax.ppermute(value, axis, [(i, (i + by) % size) for i in range(size)])


def partial_scores(queries, span):
    return lax.dot_general(
        queries,
        span.astype(jnp.float32),
        (((1,), (1,)), ((), ())),
        precision=lax.Precision.HIGHEST,
        preferred_element_type=jnp.float32,
    )


def lookup(table, indices):
    matches = indices[:, None] == lax.iota(jnp.int32, table.shape[0])[None, :]
    return jnp.sum(jnp.where(matches, table[None, :], 0.0), axis=1)


def on_device(query_grads, train_grads, example_ids, query_ids, query_norms, train_norms):
    visited = [(train_grads, example_ids)]
    current = train_grads
    current_ids = example_ids
    for offset in range(1, STEPS):
        current, current_ids = passed_along((current, current_ids), "query", 1)
        visited.append((current, current_ids))
    partials = [partial_scores(query_grads, span) for span, span_ids in visited]
    summed = jnp.concatenate(
        [lax.psum_scatter(piece, "dim", scatter_dimension=0, tiled=True) for piece in partials],
        axis=1,
    )
    seen_ids = jnp.concatenate([span_ids for span, span_ids in visited], axis=0)
    train_scale = lookup(train_norms, seen_ids)
    query_scale = lookup(query_norms, query_ids)
    return summed / (query_scale[:, None] * train_scale[None, :])


def kernel(
    sizes, width, wide,
    q_ref, t_ref, eid_hbm, qid_hbm, qn_hbm, tn_hbm, out_ref,
    qf, eid_ref, qid_ref, qn_ref, tn_ref, code, tb, acc, scales, tiles, tiles_in,
    local_sem, own_send, fwd_send, q_recv, t_send, t_recv,
    scale_send, scale_recv, tile_send, tile_recv,
):
    groups, steps, dims = sizes
    rows = q_ref.shape[0]
    mine = rows // dims
    half = qf.shape[1]
    chunks = half // width
    y, z, d = lax.axis_index("groups"), lax.axis_index("query"), lax.axis_index("dim")
    other_y = 1 - y
    high = z // 2
    is_inner = jnp.logical_or(z == 1, z == 2)
    partner = jnp.where(high == 0, 1 - z, 5 - z)
    end = jnp.where(high == 0, 0, 3)
    far_inner = jnp.where(high == 0, 2, 1)
    far_end = jnp.where(high == 0, 3, 0)
    plane = groups * dims
    in_plane = y * dims + d

    def cols(c, base=0):
        return pl.ds(pl.multiple_of(base + c * width, width), width)

    def remote(src, dst, send, recv, to):
        return pltpu.make_async_remote_copy(
            src_ref=src, dst_ref=dst, send_sem=send, recv_sem=recv,
            device_id=to, device_id_type=MESH,
        )

    def send_code(block, c, to_z, send):
        view = code.at[block, :, cols(c)]
        return remote(view, view, send, q_recv.at[block, c], (y, to_z, d))

    def got_code(block, c):
        send_code(block, c, partner, own_send.at[0, c]).wait_recv()

    def send_train(c, half_of, slot, send, to):
        return remote(
            t_ref.at[:, cols(c, half_of * half)],
            tb.at[pl.ds(pl.multiple_of(slot * rows, rows), rows), cols(c)],
            send, t_recv.at[slot, c], to,
        )

    def got_train(slot, c):
        send_train(c, y, slot, t_send.at[0, c], (y, partner, d)).wait_recv()

    across = [(c, other_y, y, t_send.at[0, c], (other_y, z, d)) for c in range(chunks)]
    diagonal = [(c, other_y, 2 + y, t_send.at[0, c], (other_y, partner, d)) for c in range(chunks)]
    straight = [(c, y, 2 + y, t_send.at[1, c], (y, partner, d)) for c in range(chunks)]

    load_q = pltpu.make_async_copy(
        q_ref.at[:, pl.ds(pl.multiple_of(y * half, half), half)], qf, local_sem.at[0])
    load_t = pltpu.make_async_copy(
        t_ref.at[:, pl.ds(pl.multiple_of(y * half, half), half)],
        tb.at[pl.ds(pl.multiple_of(y * rows, rows), rows), :], local_sem.at[1])
    load_q.start()
    load_t.start()
    tables = [
        pltpu.make_async_copy(src, dst, local_sem.at[2 + at])
        for at, (src, dst) in enumerate(
            [(eid_hbm, eid_ref), (qid_hbm, qid_ref), (qn_hbm, qn_ref), (tn_hbm, tn_ref)])
    ]
    for table in tables:
        table.start()

    barrier = pltpu.get_barrier_semaphore()
    peers = []
    for step in range(1, plane):
        at = lax.rem(in_plane + step, plane)
        peers.append((at // dims, z, lax.rem(at, dims)))
    for step in range(1, steps):
        peers.append((y, lax.rem(z + step, steps), d))
    peers.append((other_y, partner, d))
    for peer in peers:
        pl.semaphore_signal(barrier, inc=1, device_id=peer, device_id_type=MESH)
    load_q.wait()

    def largest(c, most):
        return jnp.maximum(most, jnp.max(jnp.abs(qf[:, cols(c)]), axis=1, keepdims=True))

    top = jnp.maximum(lax.fori_loop(0, chunks, largest, jnp.zeros((rows, 1), jnp.float32)), 1e-30)
    scales[z] = jnp.broadcast_to(top * (1.0 / (FULL * FULL)), (rows, 128))
    inverse = 1.0 / top

    def encode(c):
        x = qf[:, cols(c)]
        size = (jnp.sqrt(jnp.abs(x) * inverse) * FULL + 0.5).astype(jnp.int32)
        code[z, :, cols(c)] = jnp.where(x < 0, -size, size).astype(jnp.int16)

    def send_wide(c):
        @pl.when(is_inner)
        def _():
            send_code(z, c, far_inner, own_send.at[1, c]).start()

        send_code(z, c, partner, own_send.at[0, c]).start()

    def encode_wide(c, carry):
        encode(c)
        send_wide(c)
        return carry

    encode(0)
    pl.semaphore_wait(barrier, len(peers))
    send_wide(0)
    lax.fori_loop(1, wide, encode_wide, 0)

    @pl.when(is_inner)
    def _():
        for args in across:
            send_train(*args).start()

    @pl.when(jnp.logical_not(is_inner))
    def _():
        for args in across[:wide]:
            send_train(*args).start()

    def send_scale(step):
        return remote(
            scales.at[z], scales.at[z], scale_send.at[step - 1], scale_recv.at[z],
            (y, lax.rem(z + step, steps), d))

    for step in range(1, steps):
        send_scale(step).start()

    def encode_rest(c, carry):
        encode(c)

        @pl.when(jnp.logical_not(is_inner))
        def _():
            send_code(z, c, partner, own_send.at[0, c]).start()
        return carry

    lax.fori_loop(wide, chunks, encode_rest, 0)

    def pick(table, ids):
        at = lax.broadcasted_iota(jnp.int32, (ids.shape[0], table.shape[1]), 1)
        return jnp.sum(jnp.where(at == ids, table, 0.0), axis=1, keepdims=True)

    def column(ids):
        count = ids.shape[1]
        square = (count, count)
        same = lax.broadcasted_iota(jnp.int32, square, 0) == lax.broadcasted_iota(jnp.int32, square, 1)
        wide_ids = jnp.broadcast_to(ids.astype(jnp.float32), square)
        return jnp.sum(jnp.where(same, wide_ids, 0.0), axis=1, keepdims=True).astype(jnp.int32)

    for table in tables:
        table.wait()
    train_scale = pick(tn_ref[...], column(eid_ref[...]))
    span = steps * rows
    lane = lax.broadcasted_iota(jnp.int32, (rows, 128), 1)
    own_lane = lane == lax.broadcasted_iota(jnp.int32, (rows, 128), 0) + 2 * groups * rows
    train_row = jnp.sum(jnp.where(own_lane, train_scale, 0.0), axis=0, keepdims=True)
    query_scale = pick(qn_ref[...], column(qid_ref[...]))

    acc[...] = jnp.zeros_like(acc)
    load_t.wait()

    def multiply(c, held):
        coded = code[:, :, cols(c)].reshape(steps * rows, width).astype(jnp.int32).astype(jnp.float32)
        value = coded * jnp.abs(coded)
        upper = value.astype(jnp.bfloat16)
        lower = (value - upper.astype(jnp.float32)).astype(jnp.bfloat16)
        acc[:, :held] += lax.dot_general(
            jnp.concatenate([upper, lower], axis=0), tb[:held, cols(c)],
            (((1,), (1,)), ((), ())), preferred_element_type=jnp.float32,
        )

    def multiply_block(block, c, held):
        coded = code[block, :, cols(c)].astype(jnp.int32).astype(jnp.float32)
        value = coded * jnp.abs(coded)
        upper = value.astype(jnp.bfloat16)
        lower = (value - upper.astype(jnp.float32)).astype(jnp.bfloat16)
        product = lax.dot_general(
            jnp.concatenate([upper, lower], axis=0), tb[:held, cols(c)],
            (((1,), (1,)), ((), ())), preferred_element_type=jnp.float32,
        )
        acc[pl.ds(pl.multiple_of(block * rows, rows), rows), :held] += product[:rows] + product[rows:]

    narrow = groups * rows

    around = [
        [lax.rem(at + step, size) for step in range(size)]
        for at, size in zip((y, z, d), sizes)
    ]
    peers_all = [
        (to_y, to_z, to_d)
        for at_z, to_z in enumerate(around[1])
        for at_y, to_y in enumerate(around[0])
        for at_d, to_d in enumerate(around[2])
        if at_y + at_z + at_d
    ]

    offsets_z = [
        at_z
        for at_z in range(steps)
        for at_y in range(groups)
        for at_d in range(dims)
        if at_y + at_z + at_d
    ]

    def slot(peer):
        return (peer[0] * steps + peer[1]) * dims + peer[2]

    place = slot((y, z, d))

    def send_tile(at):
        peer = peers_all[at]
        return remote(tiles.at[peer[1] * dims + peer[2]], tiles_in.at[place],
                      tile_send.at[0], tile_recv.at[0], peer)

    def got_scales():
        for step in range(1, steps):
            source = lax.rem(z + step, steps)
            remote(scales.at[source], scales.at[source], scale_send.at[0], scale_recv.at[source],
                   (y, source, d)).wait_recv()

    def give_tiles():
        for at_z in (2, 1, 3, 0):
            to_z = around[1][at_z]
            upper = acc[pl.ds(pl.multiple_of(to_z * rows, rows), rows), :]
            lower = acc[pl.ds(pl.multiple_of((steps + to_z) * rows, rows), rows), :]
            product = (upper + lower) * scales[to_z] + train_row
            for to in range(dims):
                tiles[to_z * dims + to] = product[to * mine:(to + 1) * mine]
            for at, peer_z in enumerate(offsets_z):
                if peer_z == at_z:
                    send_tile(at).start()
        tiles_in[place] = tiles[z * dims + d]

    @pl.when(jnp.logical_not(is_inner))
    def _():
        for args in straight[wide:] + diagonal[wide:]:
            send_train(*args).start()

        def visit(c, carry):
            got_code(partner, c)
            got_code(far_inner, c)
            got_code(far_end, c)
            got_train(other_y, c)
            multiply(c, narrow)
            return carry

        lax.fori_loop(0, wide, visit, 0)
        got_scales()
        give_tiles()

        def sent(c, carry):
            send_code(z, c, partner, own_send.at[0, c]).wait_send()
            return carry

        lax.fori_loop(0, chunks, sent, 0)
        for args in across[:wide] + straight[wide:] + diagonal[wide:]:
            send_train(*args).wait_send()

    @pl.when(is_inner)
    def _():
        def pass_on(c, carry):
            got_code(end, c)
            send_code(end, c, far_inner, fwd_send.at[0, c]).start()
            got_code(far_inner, c)
            send_code(far_inner, c, end, fwd_send.at[1, c]).start()
            return carry

        lax.fori_loop(0, wide, pass_on, 0)

        def rest(c, carry):
            send_code(z, c, far_inner, own_send.at[1, c]).start()
            return carry

        lax.fori_loop(wide, chunks, rest, 0)

        def visit(c, carry):
            got_code(far_end, c)
            send_code(far_end, c, end, fwd_send.at[2, c]).start()

            @pl.when(c < chunks - wide)
            def _():
                got_code(end, wide + c)
                send_code(end, wide + c, far_inner, fwd_send.at[0, wide + c]).start()

            got_train(other_y, c)
            multiply(c, narrow)
            return carry

        lax.fori_loop(0, wide, visit, 0)

        def close(c, carry):
            got_code(far_inner, c)
            got_code(far_end, c)
            got_train(other_y, c)
            got_train(2 + y, c)
            got_train(2 + other_y, c)
            multiply(c, 2 * narrow)
            return carry

        lax.fori_loop(wide, chunks - 1, close, 0)
        got_scales()
        last = chunks - 1
        got_code(far_inner, last)
        got_train(other_y, last)
        got_train(2 + y, last)
        got_train(2 + other_y, last)
        for block in (z, end, far_inner):
            multiply_block(block, last, 2 * narrow)
        got_code(far_end, last)
        multiply_block(far_end, last, 2 * narrow)
        give_tiles()

        def sent(c, carry):
            send_code(z, c, far_inner, own_send.at[1, c]).wait_send()
            send_code(end, c, far_inner, fwd_send.at[0, c]).wait_send()
            return carry

        lax.fori_loop(0, chunks, sent, 0)

        def sent_wide(c, carry):
            send_code(z, c, end, own_send.at[0, c]).wait_send()
            send_code(far_inner, c, end, fwd_send.at[1, c]).wait_send()
            send_code(far_end, c, end, fwd_send.at[2, c]).wait_send()
            return carry

        lax.fori_loop(0, wide, sent_wide, 0)
        for args in across:
            send_train(*args).wait_send()

    for step in range(1, steps):
        send_scale(step).wait_send()
    others = tiles_in.at[pl.ds(0, len(peers_all))]
    all_tiles = remote(others, others, tile_send.at[0], tile_recv.at[0], peers_all[0])
    all_tiles.wait_recv()
    by_source = tiles_in[...].reshape(groups, steps, dims, mine, 128)
    summed = jnp.sum(jnp.sum(by_source, axis=2), axis=0)

    def lanes_of(block, role):
        first = [(role * groups + g) * rows for g in range(groups)]
        return jnp.where(y == 0, block[:, first[0]:first[0] + rows], block[:, first[1]:first[1] + rows])

    raw = [lanes_of(summed[k], 0) for k in range(steps)]
    raw[0] = raw[0] + lanes_of(summed[1], 1)
    raw[3] = raw[3] + lanes_of(summed[2], 1)
    lane_block = lax.broadcasted_iota(jnp.int32, (mine, span), 1) // rows
    scores = jnp.zeros((mine, span), jnp.float32)
    for k in range(steps):
        train = tiles_in[slot((y, k, d))][:, 2 * groups * rows:2 * groups * rows + rows]
        value = raw[k] / (query_scale * train)
        here = lane_block == lax.rem(z - k + steps, steps)
        scores = scores + jnp.where(here, jnp.concatenate([value] * steps, axis=1), 0.0)
    out_ref[...] = scores

    all_tiles.wait_send()


def all_pairs(sizes, query_grads, train_grads, example_ids, query_ids, query_norms, train_norms):
    groups, steps, dims = sizes
    rows, depth = query_grads.shape
    half = depth // groups
    width = min(WIDTH, half // 8)
    chunks = half // width
    wide = (chunks * 5) // 8
    plane = groups * dims
    dma, vmem = pltpu.SemaphoreType.DMA, pltpu.VMEM
    whole = pl.BlockSpec(memory_space=pltpu.VMEM)
    in_hbm = pl.BlockSpec(memory_space=pltpu.HBM)
    return pl.pallas_call(
        functools.partial(kernel, sizes, width, wide),
        out_shape=jax.ShapeDtypeStruct((rows // dims, steps * rows), jnp.float32),
        in_specs=[in_hbm] * 6,
        out_specs=whole,
        scratch_shapes=[
            vmem((rows, half), jnp.float32),
            vmem((1, example_ids.shape[0]), jnp.int32),
            vmem((1, query_ids.shape[0]), jnp.int32),
            vmem((1, query_norms.shape[0]), jnp.float32),
            vmem((1, train_norms.shape[0]), jnp.float32),
            vmem((steps, rows, half), jnp.int16),
            vmem((2 * groups * rows, half), jnp.bfloat16),
            vmem((2 * steps * rows, 128), jnp.float32),
            vmem((steps, rows, 128), jnp.float32),
            vmem((steps * dims, rows // dims, 128), jnp.float32),
            vmem((steps * plane, rows // dims, 128), jnp.float32),
            dma((6,)),
            dma((2, chunks)),
            dma((3, chunks)),
            dma((steps, chunks)),
            dma((2, chunks)),
            dma((2 * groups, chunks)),
            dma((steps - 1,)),
            dma((steps,)),
            dma((1,)),
            dma((1,)),
        ],
        compiler_params=pltpu.CompilerParams(
            collective_id=0, has_side_effects=True, vmem_limit_bytes=60 * 1024 * 1024),
    )(
        query_grads, train_grads, example_ids.reshape(1, -1), query_ids.reshape(1, -1),
        query_norms.reshape(1, -1), train_norms.reshape(1, -1),
    )


def solution(mesh):
    in_specs = (
        P("query", "dim"),
        P(("groups", "query"), "dim"),
        P(("groups", "query")),
        P(("query", "dim")),
        P(),
        P("groups"),
    )
    out_specs = P(("groups", "query", "dim"), None)
    sizes = tuple(mesh.shape[axis] for axis in ("groups", "query", "dim"))
    body = functools.partial(all_pairs, sizes) if sizes[:2] == (2, STEPS) else on_device
    return jax.shard_map(
        body, mesh=mesh, in_specs=in_specs, out_specs=out_specs, check_vma=False
    )
```
